256 devices in a mesh: rep: 8 (over z), row: 2 (over y_lo), col: 16 (over x, y_hi, core).
Axes of the slice: x: 4, y: 4 (y_hi: 2, y_lo: 2; y = y_hi * 2 + y_lo), z: 8, core: 2. Of those that a mesh axis runs over, the one named last changes fastest.
Arguments:
- inputs: bfloat16 [8, 768, 6144], P('rep', 'col', 'row'), may hold values from -6 to 6
- pre_act: bfloat16 [8, 768, 12288], P('rep', 'row', 'col'), may hold values from -6 to 6
- out_grad: bfloat16 [8, 768, 6144], P('rep', 'col', 'row'), may hold values from -6 to 6
- w_down: bfloat16 [8, 12288, 6144], P('rep', 'col', 'row'), may hold values from -0.0546875 to 0.0546875
- q_up: bfloat16 [12288, 64], P('col'), may hold values from -6 to 6
- q_down: bfloat16 [6144, 64], P('row'), may hold values from -6 to 6
Outputs:
- p_up_out: float32 [6144, 64], P('row')
- q_up_out: float32 [12288, 64], P('col')
- p_down_out: float32 [12288, 64], P('col')
- q_down_out: float32 [6144, 64], P('row')
The draws below stay inside these ranges and needn't reach their ends.
All inputs are finite; a program needn't handle non-finite values.
Results may differ from the reference program's by a relative error of at most 0.005.
Values may be sent and summed in bfloat16 or wider, within the bound.
No kernel may reach another device: no remote copies, remote signals or barrier semaphores. Data moves between devices by JAX's collectives and lax.ppermute only.
A program may use at most 128 MiB of HBM per device.

```python
import math
import jax
import jax.numpy as jnp
from jax import lax

D = 6144
FF = 12288
RANK = 64
TOKENS = 768
REPS = 8


def block_levels(stream_key, shape, split, smallest, high):
    def one(dim, blocks):
        draws = jax.random.uniform(jax.random.fold_in(jax.random.fold_in(stream_key, 6), dim), (blocks,), jnp.float32, smallest / len(split), high / len(split))
        return jnp.repeat(jnp.exp(draws), shape[dim] // blocks).reshape((-1,) + (1,) * (len(shape) - dim - 1))

    level = one(*split[0])
    for cut in split[1:]:
        level = level * one(*cut)
    return level


def bell_draw(own_key, dims, scale, limit, split=(), kind=jnp.bfloat16):
    drawn = jax.random.normal(own_key, dims, jnp.float32) * scale
    if len(split) > 0:
        drawn = block_levels(own_key, dims, split, -0.22, 0.18) * drawn
    return jnp.clip(drawn, min=-limit, max=limit).astype(kind)


def setup_inputs(seed: int = 0) -> dict:
    splits = jax.random.split(jax.random.key(seed), 7)
    inputs = bell_draw(splits[0], (REPS, TOKENS, D), 1.0, 6.0, ((0, 8), (1, 16), (2, 2)))
    pre_act = bell_draw(splits[1], (REPS, TOKENS, FF), 1.0, 6.0, ((0, 8), (1, 2), (2, 16)))
    out_grad = bell_draw(splits[2], (REPS, TOKENS, D), 1.0, 6.0, ((0, 8), (1, 16), (2, 2)))
    w_down = bell_draw(splits[3], (REPS, FF, D), FF ** -0.5, 0.0546875, ((0, 8), (1, 16), (2, 2)))
    q_up = bell_draw(splits[4], (FF, RANK), 1.0, 6.0, ((0, 16),))
    q_down = bell_draw(splits[5], (D, RANK), 1.0, 6.0, ((0, 2),))
    return dict(inputs=inputs, pre_act=pre_act, out_grad=out_grad, w_down=w_down, q_up=q_up, q_down=q_down)


def gelu_value(v):
    return 0.5 * v * (1.0 + lax.erf(v / math.sqrt(2.0)))

def gelu_slope(v):
    return 0.5 * (1.0 + lax.erf(v / math.sqrt(2.0))) + v * jnp.exp(-0.5 * v * v) / math.sqrt(2.0 * math.pi)

def orthonormal(factor):
    gram = jnp.dot(factor.T.astype(jnp.float32), factor.astype(jnp.float32), precision=lax.Precision.HIGHEST, preferred_element_type=jnp.float32)
    lower = jnp.linalg.cholesky(gram)
    return lax.linalg.triangular_solve(lower, factor, left_side=False, lower=True, transpose_a=True)

def reference(inputs, pre_act, out_grad, w_down, q_up, q_down):
    scale = 1.0 / math.sqrt(TOKENS)
    grads_up = []
    grads_down = []
    p_up = jnp.zeros((D, RANK), jnp.float32)
    p_down = jnp.zeros((FF, RANK), jnp.float32)
    for group in range(REPS):
        pre = pre_act[group].astype(jnp.float32)
        act = gelu_value(pre).astype(jnp.bfloat16)
        dact = jnp.dot(out_grad[group].astype(jnp.float32), w_down[group].T.astype(jnp.float32), preferred_element_type=jnp.float32)
        dpre = (dact * gelu_slope(pre)).astype(jnp.bfloat16)
        grad_down = (jnp.dot(act.T.astype(jnp.float32), out_grad[group].astype(jnp.float32), preferred_element_type=jnp.float32) * scale).astype(jnp.bfloat16)
        grad_up = (jnp.dot(inputs[group].T.astype(jnp.float32), dpre.astype(jnp.float32), preferred_element_type=jnp.float32) * scale).astype(jnp.bfloat16)
        p_up = p_up + jnp.dot(grad_up.astype(jnp.float32), q_up.astype(jnp.float32), preferred_element_type=jnp.float32)
        p_down = p_down + jnp.dot(grad_down.astype(jnp.float32), q_down.astype(jnp.float32), preferred_element_type=jnp.float32)
        grads_up.append(grad_up)
        grads_down.append(grad_down)
    p_up = p_up / REPS
    p_down = p_down / REPS
    hat_up = orthonormal(p_up)
    hat_down = orthonormal(p_down)
    low_up = hat_up.astype(jnp.bfloat16)
    low_down = hat_down.astype(jnp.bfloat16)
    q_up_new = jnp.zeros((FF, RANK), jnp.float32)
    q_down_new = jnp.zeros((D, RANK), jnp.float32)
    for group in range(REPS):
        q_up_new = q_up_new + jnp.dot(grads_up[group].T.astype(jnp.float32), low_up.astype(jnp.float32), preferred_element_type=jnp.float32)
        q_down_new = q_down_new + jnp.dot(grads_down[group].T.astype(jnp.float32), low_down.astype(jnp.float32), preferred_element_type=jnp.float32)
    return (hat_up * math.sqrt(D), q_up_new / REPS, hat_down * math.sqrt(FF), q_down_new / REPS)
```

```python
import math

import jax
import jax.numpy as jnp
from jax import lax
from jax.experimental import pallas as pl
from jax.experimental.pallas import tpu as pltpu
from jax.sharding import PartitionSpec as P

D = 6144
FF = 12288
RANK = 64
COLS = 16
F32 = jnp.float32
BF16 = jnp.bfloat16

CORE = [(i, i ^ 1) for i in range(COLS)]
YHI = [(i, i ^ 2) for i in range(COLS)]
X_UP = [(i, (i + 4) % COLS) for i in range(COLS)]
X_DOWN = [(i, (i + 12) % COLS) for i in range(COLS)]
ROW = [(0, 1), (1, 0)]


def gather_col(own, place):
    across = lax.ppermute(own, "col", YHI)
    prev = lax.ppermute(own, "col", X_UP)
    succ = lax.ppermute(own, "col", X_DOWN)
    up = lax.ppermute(jnp.concatenate([prev[:32], across], axis=0), "col", X_UP)
    down = lax.ppermute(jnp.concatenate([succ[32:], across], axis=0), "col", X_DOWN)
    last_up = lax.ppermute(up[32:48], "col", X_UP)
    last_down = lax.ppermute(down[32:64], "col", X_DOWN)
    parts = [own, prev, succ, across, up, down, last_up, last_down]
    parts += [lax.ppermute(part, "col", CORE) for part in parts]
    return assemble(place, parts), across


PIECES = [
    [(0, 48, (0, 0), 0)],
    [(0, 48, (-1, 0), 0)],
    [(0, 48, (1, 0), 0)],
    [(0, 48, (0, 1), 0)],
    [(0, 32, (2, 0), 0), (32, 48, (-1, 1), 0)],
    [(0, 16, (2, 0), 32), (16, 48, (1, 1), 0)],
    [(0, 16, (2, 1), 0)],
    [(0, 32, (2, 1), 16)],
]
MOVES = [
    (8 * core + part, first, rows, spot, core, within)
    for core in (0, 1)
    for part, pieces in enumerate(PIECES)
    for first, rows, spot, within in pieces
]
SPOTS = sorted({(move[3], move[4]) for move in MOVES})


def assemble_kernel(place_ref, *refs):
    parts, whole = refs[:16], refs[16]
    for part, first, rows, spot, core, within in MOVES:
        start = place_ref[SPOTS.index((spot, core))] * 48 + within
        whole[pl.ds(pl.multiple_of(start, 16), rows), :] = parts[part][first : first + rows, :]


def assemble(place, parts):
    vmem = pl.BlockSpec(memory_space=pltpu.VMEM)
    return pl.pallas_call(
        assemble_kernel,
        in_specs=[pl.BlockSpec(memory_space=pltpu.SMEM)] + [vmem] * 16,
        out_specs=vmem,
        out_shape=jax.ShapeDtypeStruct((768, parts[0].shape[1]), BF16),
        compiler_params=pltpu.CompilerParams(vmem_limit_bytes=24 * 2**20),
    )(place, *parts)


def inverse_kernel(gram_ref, out_ref):
    shape = (RANK, 2 * RANK)
    i = lax.broadcasted_iota(jnp.int32, shape, 0)
    j = lax.broadcasted_iota(jnp.int32, shape, 1)
    both = jnp.concatenate([gram_ref[...], jnp.zeros((RANK, RANK), F32)], axis=1)
    both = jnp.where(j == i + RANK, 1.0, both)
    diagonal = jnp.ones((RANK, 1), F32)
    sub = lax.broadcasted_iota(jnp.int32, (RANK, 1), 0)
    for k in range(RANK):
        column = both[:, k : k + 1]
        pivot = both[k : k + 1, k : k + 1]
        diagonal = jnp.where(sub == k, pivot, diagonal)
        factor = jnp.where(sub > k, column / pivot, 0.0)
        both = both - factor * both[k : k + 1, :]
    out_ref[...] = (both / jnp.sqrt(diagonal))[:, RANK:]


def inverse_factor(gram):
    return pl.pallas_call(
        inverse_kernel, out_shape=jax.ShapeDtypeStruct((RANK, RANK), F32)
    )(gram)


def gelu_kernel(place_ref, pre_ref, act_ref, slope_ref):
    v = pre_ref[0].astype(F32)
    phi = 0.5 * (1.0 + lax.erf(v * (1.0 / math.sqrt(2.0))))
    act_ref[0] = (v * phi).astype(BF16)
    slope_ref[0] = phi + v * jnp.exp(-0.5 * v * v) * (1.0 / math.sqrt(2.0 * math.pi))


def gelu_blocks(place, pre):
    blocks, rows, cols = pre.shape
    moved = pl.BlockSpec((1, rows, cols), lambda i, place: (place[i], 0, 0))
    here = pl.BlockSpec((1, rows, cols), lambda i, place: (i, 0, 0))
    return pl.pallas_call(
        gelu_kernel,
        grid_spec=pltpu.PrefetchScalarGridSpec(
            num_scalar_prefetch=1, grid=(blocks,), in_specs=[moved], out_specs=[here, here]
        ),
        out_shape=[
            jax.ShapeDtypeStruct(pre.shape, BF16),
            jax.ShapeDtypeStruct(pre.shape, F32),
        ],
    )(place, pre)


def nn(a, b):
    return lax.dot_general(a, b, (((1,), (0,)), ((), ())), preferred_element_type=F32)


def nt(a, b):
    return lax.dot_general(a, b, (((1,), (1,)), ((), ())), preferred_element_type=F32)


def split(a):
    high = lax.reduce_precision(a, 8, 7)
    return jnp.concatenate([high.astype(BF16), (a - high).astype(BF16)], axis=0)


def fold(a):
    return a[:RANK] + a[RANK:]


def exact(a, b, dims):
    return lax.dot_general(
        a, b, (dims, ((), ())), precision=lax.Precision.HIGHEST, preferred_element_type=F32
    )


def exchange(pieces, axes):
    return lax.all_to_all(pieces, axes, 0, 0, tiled=True)


def spread(piece, axes, count):
    return exchange(jnp.broadcast_to(piece[None], (count,) + piece.shape), axes)


def pack(a):
    wide = a.shape[1] // 2
    return jnp.concatenate([a[:, :wide], a[:, wide:]], axis=0).reshape(16, 8, wide)


def unpack(a):
    a = a.reshape(2 * RANK, a.shape[-1])
    return jnp.concatenate([a[:RANK], a[RANK:]], axis=1)


def sum_rep_row(part):
    mine = exchange(pack(part), ("rep", "row")).sum(axis=0)
    return unpack(spread(mine, ("rep", "row"), 16))


def pick(flag, a, b):
    return jnp.where(flag, a, b), jnp.where(flag, b, a)


def per_device(inputs, pre_act, out_grad, w_down, q_up, q_down):
    groups = 8
    scale = 1.0 / (math.sqrt(768.0) * groups)
    row = lax.axis_index("row")
    col = lax.axis_index("col")
    x, y_hi, core = col // 4, (col // 2) % 2, col % 2
    place = jnp.stack(
        [((x + dx) % 4) * 4 + (y_hi ^ dy) * 2 + (core ^ dc) for (dx, dy), dc in SPOTS]
    ).astype(jnp.int32)

    grads, arrived = gather_col(out_grad[0], place)
    rows = lax.all_gather(inputs[0], "col", axis=0, tiled=True)

    u = nn(out_grad[0], q_down)
    high = lax.reduce_precision(u, 8, 7)
    u = jnp.concatenate([high.astype(BF16), (u - high).astype(BF16)], axis=1)
    u = spread(u, ("row", "col"), 32).reshape(2, 768, 2 * RANK)
    u = lax.dynamic_slice(u, (0, row * 384, 0), (2, 384, 2 * RANK))
    u = jnp.concatenate([u[0], u[1]], axis=1)
    own = pre_act[0].astype(F32)
    act_own = (0.5 * own * (1.0 + lax.erf(own * (1.0 / math.sqrt(2.0))))).astype(BF16)
    p_down = lax.dot_general(u, act_own, (((0,), (0,)), ((), ())), preferred_element_type=F32)
    p_down = sum_rep_row(fold(p_down[: 2 * RANK] + p_down[2 * RANK :]) * scale)
    gram_down = exact(p_down, p_down, ((1,), (1,)))
    gram_down = jnp.concatenate([gram_down[:32], gram_down[32:]], axis=1)
    gram_down = spread(gram_down, "col", 16).sum(axis=0)
    gram_down = jnp.concatenate([gram_down[:, :RANK], gram_down[:, RANK:]], axis=0)
    inverse_down = inverse_factor(gram_down)
    p_hat_down = exact(inverse_down, p_down, ((1,), (0,)))

    own_pre, _ = lax.optimization_barrier((pre_act[0], arrived))
    pre_other = lax.ppermute(own_pre, "row", ROW)
    pre_all = jnp.concatenate([own_pre, pre_other], axis=0).reshape(16, 48, 768)
    act, slope = gelu_blocks(jnp.arange(16, dtype=jnp.int32) ^ (row * 8), pre_all)
    act = act.reshape(768, 768)
    slope = slope.reshape(768, 768)

    dact = nt(grads, w_down[0])
    dpre = (dact * slope).astype(BF16)
    z_part = nt(q_up.T, dpre)
    z = z_part + lax.ppermute(z_part, "row", ROW)

    s = nt(p_hat_down.astype(BF16), act)
    q_part = fold(nn(split(s), grads))
    p_part = fold(nn(split(z), rows)) * scale
    first = core == 0
    mine, other = pick(first, p_part, q_part)
    mine = mine + lax.ppermute(other.astype(BF16), "col", CORE).astype(F32)
    chips = [[2 * i + k for i in range(8)] for k in (0, 1)]
    mine = lax.all_to_all(
        mine.astype(BF16).reshape(8, 8, 3072), "col", 0, 0, tiled=True, axis_index_groups=chips
    )
    mine = mine.astype(F32).sum(axis=0).astype(BF16)
    mine = spread(mine, "rep", 8).astype(F32).sum(axis=0).astype(BF16)
    mine = lax.all_to_all(
        jnp.broadcast_to(mine[None], (8, 8, 3072)), "col", 0, 0, tiled=True, axis_index_groups=chips
    ).reshape(RANK, 3072)
    p_up, q_down_raw = pick(first, mine, lax.ppermute(mine, "col", CORE))

    w_part = nt(p_up, rows)
    w = w_part + lax.ppermute(w_part, "row", ROW)
    y = sum_rep_row(fold(nn(split(w), dpre)))

    p_up = p_up.astype(F32)
    gram_up = exact(p_up, p_up, ((1,), (1,)))
    gram_up = gram_up + lax.ppermute(gram_up, "row", ROW)
    inverse_up = inverse_factor(gram_up)
    dims = ((1,), (0,))
    p_up_out = exact(inverse_up * math.sqrt(D), p_up, dims)
    q_up_out = exact(inverse_up * scale, y, dims)
    p_down_out = p_hat_down * math.sqrt(FF)
    q_down_out = q_down_raw.astype(F32) * scale
    return p_up_out.T, q_up_out.T, p_down_out.T, q_down_out.T


def solution(mesh):
    placed = (
        P("rep", "col", "row"),
        P("rep", "row", "col"),
        P("rep", "col", "row"),
        P("rep", "col", "row"),
        P("col", None),
        P("row", None),
    )
    return jax.shard_map(
        per_device,
        mesh=mesh,
        in_specs=placed,
        out_specs=(P("row", None), P("col", None), P("col", None), P("row", None)),
        check_vma=False,
    )
```
